32 devices in a mesh: grp: 8 (over z, x), tp: 4 (over y, core).
Axes of the slice: x: 2, y: 2, z: 4, core: 2. Of those that a mesh axis runs over, the one named last changes fastest.
Arguments:
- thinker_rows: bfloat16 [2048, 8192], P(('grp', 'tp')), may hold values from -6 to 6
- norm_gain: bfloat16 [8192], replicated, may hold values from 0.5 to 1.5
- w_query: bfloat16 [8192, 4096], P(None, 'tp'), may hold values from -0.0625 to 0.0625
- w_key: bfloat16 [8192, 1024], P(None, 'tp'), may hold values from -0.0625 to 0.0625
- w_value: bfloat16 [8192, 1024], P(None, 'tp'), may hold values from -0.0625 to 0.0625
- w_out: bfloat16 [4096, 8192], P('tp'), may hold values from -0.75 to 0.75
- cache_keys: bfloat16 [128, 320, 1024], P('grp', None, 'tp'), may hold values from -576 to 576
- cache_values: bfloat16 [128, 320, 1024], P('grp', None, 'tp'), may hold values from -6 to 6
- session_ids: int32 [8, 256], P('grp'), may hold values from 0 to 15, never falling along the last dimension, each value on 1 to 20 neighbouring positions
- cache_lens: int32 [8, 16], P('grp'), may hold values from 1 to 320, 3200 in all within a row
- owners: int32 [128, 1], P('grp'), may hold values from 0 to 7; in each aligned block of 16 rows (0 to 15, 16 to 31, ...) at most 2 rows name the same one
- talker_gain: bfloat16 [8192], replicated, may hold values from 0.5 to 1.5
- w_talker: bfloat16 [8192, 1024], P(None, 'tp'), may hold values from -0.0625 to 0.0625
Outputs:
- talker_rows: bfloat16 [2560, 1024], P('grp', 'tp')
The draws below stay inside these ranges and needn't reach their ends.
Inputs may be any that keep to these rules, and one draw needn't show every extreme that they name: `session_ids`: within a group the ids never fall; every one of the 16 sessions has 1 to 20 tokens and some session exactly 20. `cache_lens`: some session of every group has exactly 320 live slots. `owners`: of one group's 16 sessions at most 2 have the same owner, and some owner has exactly 2 of some group.
All inputs are finite; a program needn't handle non-finite values.
Results may differ from the reference program's by a relative error of at most 0.017.
The reference program's roundings to bfloat16 on the way count: a program that leaves them out, or rounds other values in their place, can miss the bound.
Values may be sent and summed in bfloat16 or wider, within the bound.
A program may use at most 128 MiB of HBM per device.

```python
import math
import jax
import jax.numpy as jnp
import numpy as np
from jax import lax

D = 8192
HEADS = 32
KV_HEADS = 8
HEAD_DIM = 128
TW = 1024
SESS = 16
CACHE = 320
CAPS = 2
TOK = 256
GQA = 4
MOST = 20
TOKENS = 2048
SESSIONS = 128
TROWS = 2560
N_GRP = 8


def draw_cache_keys(key, part):
    base = jnp.clip(jax.random.normal(key, (SESSIONS, CACHE, KV_HEADS * HEAD_DIM), jnp.float32), -6.0, 6.0)
    return base.astype(jnp.bfloat16)


def levels(key, shape, shards, low, top_value):
    loudness = 1.0
    for dim, shards_of in shards:
        draws = jax.random.uniform(jax.random.fold_in(jax.random.fold_in(key, 6), dim), (shards_of,), jnp.float32, low / len(shards), top_value / len(shards))
        loudness = loudness * jnp.repeat(jnp.exp(draws), shape[dim] // shards_of).reshape((-1,) + (1,) * (len(shape) - 1 - dim))
    return loudness


def split_up(amount, total, most, lean):
    portions = [(1 << 20) // math.isqrt(rank ** lean) + 1 for rank in range(2, amount + 1)]
    surplus, holding = total - most - (amount - 1), [1] * (amount - 1)
    while surplus > 0:
        movable = [i for i in range(amount - 1) if holding[i] < most]
        whole, remaining = sum([portions[i] for i in movable]), surplus
        for i in movable:
            more = min(most - holding[i], max(1, remaining * portions[i] // whole), surplus)
            holding[i] = holding[i] + more
            surplus = surplus - more
    return np.array([most] + holding)


def uneven(own_key, number_of, total, most, skew):
    if number_of == 2:
        one = jax.random.randint(own_key, (), max(1, total - most), min(most, total - 1) + 1)
        return jnp.stack([one, total - one])
    lengths = jnp.asarray(split_up(number_of, total, most, skew), jnp.int32)
    pairs = (number_of - 1) // 2
    donor, taker = lengths[1:1 + 2 * pairs:2], lengths[2:2 + 2 * pairs:2]
    margin = jnp.minimum(donor - 1, most - taker)
    passed = jax.random.randint(jax.random.fold_in(own_key, 1), (pairs,), 0, 1 << 20) % (margin + 1)
    lengths = lengths.at[1:1 + 2 * pairs:2].set(donor - passed).at[2:2 + 2 * pairs:2].set(taker + passed)
    return lengths[jax.random.permutation(jax.random.fold_in(own_key, 2), number_of)]


def assign_block(own_key, own, number, rows, number_of, top, bound, skew):
    order = jax.random.permutation(own_key, number_of)
    heavy_load, ordinary = load_shares(number_of, rows * top, bound, skew, True), load_shares(number_of, rows * top, bound, skew, False)
    places = jnp.arange(number_of)

    def named(lengths, offset_by):
        used = int((lengths > 0).sum())
        fixed = max(1, used // 4)
        moved = fixed + (places - fixed + offset_by * (used - fixed)) % max(1, number_of - fixed)
        return jnp.zeros((number_of,), jnp.int32).at[order[jnp.where(places < fixed, places, moved)]].set(jnp.asarray(lengths, jnp.int32))

    lengths = jnp.where(number % 4 == 0, named(heavy_load, number // 4), named(ordinary, number - number // 4 - 1))
    mixed = jax.random.permutation(jax.random.fold_in(own, 3), number_of)
    source_of, sink = mixed[0:number_of // 2 * 2:2], mixed[1:number_of // 2 * 2:2]
    margin = jnp.minimum(lengths[source_of] - 1, bound - lengths[sink]) // 2
    margin = jnp.where((source_of == order[0]) | (sink == order[0]) | (lengths[sink] == 0), 0, jnp.maximum(margin, 0))
    moved = jax.random.randint(jax.random.fold_in(own, 4), (number_of // 2,), 0, 1 << 20) % (margin + 1)
    lengths = lengths.at[source_of].add(-moved).at[sink].add(moved)
    members = jnp.searchsorted(jnp.cumsum(lengths), jnp.arange(rows * top), side="right").astype(jnp.int32)
    listing = members.reshape(top, rows).T
    listing = listing[jax.random.permutation(jax.random.fold_in(own, 1), rows)]
    offset_by = jax.random.randint(jax.random.fold_in(own, 2), (rows, 1), 0, top)
    return jnp.take_along_axis(listing, (jnp.arange(top)[None, :] + offset_by) % top, axis=1)


def load_shares(count, total, most, skew, full):
    portions = [(1 << 20) // math.isqrt(rank ** skew) + 1 for rank in range(1, count + 1)]
    largest = most if full else min(most, max(-(-total // count), total * portions[0] // sum(portions)))
    least = 1 if total - largest >= count - 1 else 0
    holding, rest = [largest] + [least] * (count - 1), total - largest - least * (count - 1)
    while rest > 0:
        free = [i for i in range(1, count) if holding[i] < largest] or [i for i in range(1, count) if holding[i] < most]
        pool, remaining = sum([portions[i] for i in free]), rest
        for i in free:
            addition = min(most - holding[i], max(1, remaining * portions[i] // pool), rest)
            holding[i] = holding[i] + addition
            rest = rest - addition
    return np.array(holding)


def gaussian(stream_key, extent, deviation, bound, shards=(), kind=jnp.bfloat16):
    array = jax.random.normal(stream_key, extent, jnp.float32) * deviation
    if len(shards) > 0:
        array = levels(stream_key, extent, shards, -0.22, 0.18) * array
    return jnp.clip(array, min=-bound, max=bound).astype(kind)


def setup_inputs(seed: int = 0) -> dict:
    key_of = jax.random.split(jax.random.key(seed), 14)
    thinker_rows = gaussian(key_of[0], (TOKENS, D), 1.0, 6.0, ((0, 32),))
    norm_gain = jnp.clip(1.0 + 0.1 * jax.random.normal(key_of[1], (D,), jnp.float32), 0.5, 1.5).astype(jnp.bfloat16)
    w_query = gaussian(key_of[2], (D, HEADS * HEAD_DIM), D ** -0.5, 0.0625, ((1, 4),))
    w_key = gaussian(key_of[3], (D, KV_HEADS * HEAD_DIM), D ** -0.5, 0.0625, ((1, 4),))
    w_value = gaussian(key_of[4], (D, KV_HEADS * HEAD_DIM), D ** -0.5, 0.0625, ((1, 4),))
    w_out = gaussian(key_of[5], (HEADS * HEAD_DIM, D), (HEADS * HEAD_DIM // 64) ** -0.5, 0.75, ((0, 4),))
    cache_keys = draw_cache_keys(jax.random.fold_in(key_of[13], 71), 0)
    cache_values = gaussian(key_of[7], (SESSIONS, CACHE, KV_HEADS * HEAD_DIM), 1.0, 6.0, ((0, 8), (2, 4)))
    session_ids = jax.vmap(lambda own: jnp.searchsorted(jnp.cumsum(uneven(own, SESS, TOK, MOST, 1)), jnp.arange(TOK), side="right"))(jax.random.split(key_of[8], N_GRP)).reshape((N_GRP, TOK)).astype(jnp.int32)
    cache_lens = jax.vmap(lambda own: uneven(own, SESS, SESS * CACHE * 5 // 8, CACHE, 1))(jax.random.split(key_of[9], N_GRP)).reshape((N_GRP, SESS)).astype(jnp.int32)
    owners_keys = jax.random.split(jax.random.fold_in(key_of[10], 1), SESSIONS // SESS)
    owners_turns = jax.random.permutation(jax.random.fold_in(key_of[10], 3), SESSIONS // SESS)
    owners = jax.vmap(lambda own, number: assign_block(jax.random.fold_in(key_of[10], 2), own, number, SESS, N_GRP, 1, CAPS, 2))(owners_keys, owners_turns).reshape((SESSIONS, 1))
    talker_gain = jnp.clip(1.0 + 0.1 * jax.random.normal(key_of[11], (D,), jnp.float32), 0.5, 1.5).astype(jnp.bfloat16)
    w_talker = gaussian(key_of[12], (D, TW), D ** -0.5, 0.0625, ((1, 4),))
    return {"thinker_rows": thinker_rows, "norm_gain": norm_gain, "w_query": w_query, "w_key": w_key, "w_value": w_value, "w_out": w_out, "cache_keys": cache_keys, "cache_values": cache_values, "session_ids": session_ids, "cache_lens": cache_lens, "owners": owners, "talker_gain": talker_gain, "w_talker": w_talker}


EPSILON = 1e-06

def rms_scaled(values, weights):
    floats = values.astype(jnp.float32)
    mean_square = lax.optimization_barrier(jnp.mean(floats * floats, axis=-1, keepdims=True))
    return (floats * lax.rsqrt(mean_square + EPSILON) * weights.astype(jnp.float32)).astype(jnp.bfloat16)

def slot_tables(session_row, owner_row):
    session_range = jnp.arange(SESS, dtype=jnp.int32)
    member = (session_row[:, None] == session_range[None, :]).astype(jnp.int32)
    counts = lax.optimization_barrier(jnp.sum(member, axis=0))
    starts = jnp.cumsum(counts) - counts
    first_row = lax.optimization_barrier(jnp.sum(member * starts[None, :], axis=1))
    position = jnp.arange(session_row.shape[0], dtype=jnp.int32) - first_row
    earlier = (owner_row[:, None] == owner_row[None, :]) & (session_range[None, :] < session_range[:, None])
    owner_rank = lax.optimization_barrier(jnp.sum(earlier.astype(jnp.int32), axis=1))
    owner_slot = owner_row * CAPS + owner_rank
    destination = lax.optimization_barrier(jnp.sum(member * owner_slot[None, :], axis=1)) * MOST + position
    slot_index = session_row * MOST + position
    return (counts, slot_index, destination)

def attend(q_slots, k_slots, v_slots, cache_k, cache_v, live_lens, counts):
    score_scale = HEAD_DIM ** (-0.5)
    cached = jnp.einsum('smkgd,sckd->skgmc', q_slots.astype(jnp.float32), cache_k.astype(jnp.float32)) * score_scale
    fresh = jnp.einsum('smkgd,snkd->skgmn', q_slots.astype(jnp.float32), k_slots.astype(jnp.float32)) * score_scale
    live_cache = jnp.arange(cache_k.shape[1], dtype=jnp.int32)[None, :] < live_lens[:, None]
    places = jnp.arange(MOST, dtype=jnp.int32)
    causal = places[None, :] <= places[:, None]
    live_fresh = causal[None, :, :] & (places[None, None, :] < counts[:, None, None])
    cached = jnp.where(live_cache[:, None, None, None, :], cached, -1e+30)
    fresh = jnp.where(live_fresh[:, None, None, :, :], fresh, -1e+30)
    highest = jnp.maximum(lax.optimization_barrier(jnp.max(cached, axis=-1)), lax.optimization_barrier(jnp.max(fresh, axis=-1)))
    exp_cached = jnp.exp(cached - highest[..., None])
    exp_fresh = jnp.exp(fresh - highest[..., None])
    denominator = lax.optimization_barrier(jnp.sum(exp_cached, axis=-1)) + lax.optimization_barrier(jnp.sum(exp_fresh, axis=-1))
    weight_cached = (exp_cached / denominator[..., None]).astype(jnp.bfloat16)
    weight_fresh = (exp_fresh / denominator[..., None]).astype(jnp.bfloat16)
    mixed = jnp.einsum('skgmc,sckd->smkgd', weight_cached.astype(jnp.float32), cache_v.astype(jnp.float32))
    mixed = mixed + jnp.einsum('skgmn,snkd->smkgd', weight_fresh.astype(jnp.float32), v_slots.astype(jnp.float32))
    return mixed.astype(jnp.bfloat16)

def reference(thinker_rows, norm_gain, w_query, w_key, w_value, w_out, cache_keys, cache_values, session_ids, cache_lens, owners, talker_gain, w_talker):
    slot_count = SESS * MOST
    head_width = GQA * HEAD_DIM

    def one_group(operands):
        thinker, session_row, length_row, owner_row, keys_group, values_group = operands
        normed = rms_scaled(thinker, norm_gain)
        query = jnp.dot(normed, w_query, preferred_element_type=jnp.float32).astype(jnp.bfloat16)
        key_new = jnp.dot(normed, w_key, preferred_element_type=jnp.float32).astype(jnp.bfloat16)
        value_new = jnp.dot(normed, w_value, preferred_element_type=jnp.float32).astype(jnp.bfloat16)
        counts, slot_index, destination = slot_tables(session_row, owner_row)
        placing = (slot_index[None, :] == jnp.arange(slot_count, dtype=jnp.int32)[:, None]).astype(jnp.bfloat16)
        q_slots = jnp.dot(placing, query, preferred_element_type=jnp.float32).astype(jnp.bfloat16)
        k_slots = jnp.dot(placing, key_new, preferred_element_type=jnp.float32).astype(jnp.bfloat16)
        v_slots = jnp.dot(placing, value_new, preferred_element_type=jnp.float32).astype(jnp.bfloat16)
        mixed = attend(q_slots.reshape(SESS, MOST, KV_HEADS, GQA, HEAD_DIM), k_slots.reshape(SESS, MOST, KV_HEADS, HEAD_DIM), v_slots.reshape(SESS, MOST, KV_HEADS, HEAD_DIM), keys_group, values_group, length_row, counts)
        attention_rows = jnp.dot(placing.T, mixed.reshape(slot_count, HEADS * HEAD_DIM), preferred_element_type=jnp.float32).astype(jnp.bfloat16)
        head_total = jnp.zeros((TOK, D), jnp.float32)
        for kv_index in range(KV_HEADS):
            lower = kv_index * head_width
            partial_sum = jnp.dot(attention_rows[:, lower:lower + head_width], w_out[lower:lower + head_width], preferred_element_type=jnp.float32).astype(jnp.bfloat16)
            head_total = head_total + partial_sum.astype(jnp.float32)
        hidden = (thinker.astype(jnp.float32) + head_total).astype(jnp.bfloat16)
        routing = (destination[None, :] == jnp.arange(N_GRP * CAPS * MOST, dtype=jnp.int32)[:, None]).astype(jnp.bfloat16)
        return jnp.dot(routing, hidden, preferred_element_type=jnp.float32).astype(jnp.bfloat16).reshape(N_GRP, CAPS * MOST, D)
    sent = lax.map(one_group, (thinker_rows.reshape(N_GRP, TOK, D), session_ids, cache_lens, owners.reshape(N_GRP, SESS), cache_keys.reshape(N_GRP, SESS, CACHE, KV_HEADS, HEAD_DIM), cache_values.reshape(N_GRP, SESS, CACHE, KV_HEADS, HEAD_DIM)))
    received = jnp.transpose(sent, (1, 0, 2, 3))

    def one_owner(block_rows):
        return jnp.dot(rms_scaled(block_rows.reshape(-1, D), talker_gain), w_talker, preferred_element_type=jnp.float32).astype(jnp.bfloat16)
    return lax.map(one_owner, received).reshape(TROWS, TW)
```

```python
import functools

import jax
import jax.numpy as jnp
from jax import lax
from jax.experimental import pallas as pl
from jax.experimental.pallas import tpu as pltpu
from jax.sharding import PartitionSpec as P

HEAD_DIM = 128
SESS = 16
CAPS = 2
GQA = 4
MOST = 20
OWNER_PITCH = 48
CHUNKS = 8
VMEM_BYTES = 58 * 1024 * 1024

EPSILON = 1e-06
MESH = pl.DeviceIdType.MESH


def places(n_tp):
    me = lax.axis_index("tp")
    core = lax.rem(me, 2)
    chip = me // 2
    return me, chip, core, me + 1 - 2 * core


def greet(n_tp, n_grp=1):
    me, chip, core, sibling = places(n_tp)
    n_chips = n_tp // 2
    barrier = pltpu.get_barrier_semaphore()
    peers = [{"tp": sibling}]
    for j in range(1, n_chips):
        peers.append({"tp": lax.rem(chip + j, n_chips) * 2 + core})
    grp = lax.axis_index("grp")
    for j in range(1, n_grp):
        peers.append({"grp": lax.rem(grp + j, n_grp)})
    for peer in peers:
        pl.semaphore_signal(barrier, inc=1, device_id=peer, device_id_type=MESH)
    pl.semaphore_wait(barrier, len(peers))


def remote(src, dst, send, recv, device):
    return pltpu.make_async_remote_copy(
        src_ref=src,
        dst_ref=dst,
        send_sem=send,
        recv_sem=recv,
        device_id=device,
        device_id_type=MESH,
    )


class RowGather:
    def __init__(self, n_tp, held, sib_send, chip_send, pass_send, recv):
        self.held, self.recv = held, recv
        self.sib_send, self.chip_send, self.pass_send = sib_send, chip_send, pass_send
        self.me, self.chip, self.core, self.sibling = places(n_tp)
        self.n_chips = n_tp // 2
        self.rows = held.shape[1] // n_tp

    def block(self, f, owner):
        start = pl.multiple_of(owner * self.rows, self.rows)
        return self.held.at[f, pl.ds(start, self.rows), :]

    def copy(self, f, owner, send, target):
        ref = self.block(f, owner)
        return remote(ref, ref, send, self.recv.at[f, owner], {"tp": target})

    def partner(self, j):
        return lax.rem(self.chip + j, self.n_chips) * 2 + self.core

    def own_copies(self, f):
        copies = [
            self.copy(f, self.me, self.chip_send.at[f, j - 1], self.partner(j))
            for j in range(1, self.n_chips)
        ]
        return copies + [self.copy(f, self.me, self.sib_send.at[f], self.sibling)]

    def passed_copies(self, f):
        return [
            self.copy(f, self.partner(j), self.pass_send.at[f, j - 1], self.sibling)
            for j in range(1, self.n_chips)
        ]

    def send(self, f):
        for copy in self.own_copies(f):
            copy.start()

    def pass_on(self, f):
        for copy in self.passed_copies(f):
            copy.wait_recv()
            copy.start()

    def wait_sibling(self, f):
        self.copy(f, self.sibling, self.sib_send.at[f], self.sibling).wait_recv()
        for j in range(1, self.n_chips):
            owner = lax.rem(self.chip + j, self.n_chips) * 2 + 1 - self.core
            self.copy(f, owner, self.pass_send.at[f, j - 1], self.sibling).wait_recv()

    def wait_sends(self, f):
        for copy in self.own_copies(f) + self.passed_copies(f):
            copy.wait_send()


def gather_scratch(n_tp, rows, width):
    other = max(1, n_tp // 2 - 1)
    return [
        pltpu.VMEM((CHUNKS, n_tp * rows, width), jnp.bfloat16),
        pltpu.SemaphoreType.DMA((CHUNKS,)),
        pltpu.SemaphoreType.DMA((CHUNKS, other)),
        pltpu.SemaphoreType.DMA((CHUNKS, other)),
        pltpu.SemaphoreType.DMA((CHUNKS, n_tp)),
    ]


def column_tile(columns):
    return 512 if columns % 512 == 0 else 256 if columns % 256 == 0 else 128


def project_kernel(
    n_tp, x_ref, gain_ref, wq_ref, wk_ref, wv_ref, out_ref,
    held, sib_send, chip_send, pass_send, recv, weights, total, w_sem,
):
    width = held.shape[2]
    model_width = width * CHUNKS
    edges = [0]
    for ref in (wq_ref, wk_ref, wv_ref):
        edges.append(edges[-1] + ref.shape[1])

    def weight_copies(f):
        start = pl.multiple_of(f * width, width)
        return [
            pltpu.make_async_copy(
                ref.at[pl.ds(start, width), :],
                weights.at[f, :, pl.ds(edges[i], ref.shape[1])],
                w_sem.at[f, i],
            )
            for i, ref in enumerate((wq_ref, wk_ref, wv_ref))
        ]

    def start_weights(f, carry):
        for copy in weight_copies(f):
            copy.start()
        return carry

    lax.fori_loop(0, CHUNKS, start_weights, 0)
    greet(n_tp)
    gather = RowGather(n_tp, held, sib_send, chip_send, pass_send, recv)

    def squares(f, carry):
        part = x_ref[:, pl.ds(pl.multiple_of(f * width, width), width)].astype(jnp.float32)
        return carry + jnp.sum(part * part, axis=1, keepdims=True)

    square_sum = lax.fori_loop(
        0, CHUNKS, squares, jnp.zeros((x_ref.shape[0], 1), jnp.float32)
    )
    scale = lax.rsqrt(square_sum / model_width + EPSILON)
    rows = gather.rows

    def normalise(f, carry):
        columns = pl.ds(pl.multiple_of(f * width, width), width)
        part = x_ref[:, columns].astype(jnp.float32) * scale
        part = part * gain_ref[:, columns].astype(jnp.float32)
        start = pl.multiple_of(gather.me * rows, rows)
        held[f, pl.ds(start, rows), :] = part.astype(jnp.bfloat16)
        gather.send(f)
        return carry

    lax.fori_loop(0, CHUNKS, normalise, 0)
    total[...] = jnp.zeros_like(total)
    tile = column_tile(total.shape[1])

    def step(f, carry):
        @pl.when(f < CHUNKS)
        def _():
            gather.pass_on(f)

        @pl.when(f >= 1)
        def _():
            g = f - 1
            gather.wait_sibling(g)
            for copy in weight_copies(g):
                copy.wait()
            for lower in range(0, total.shape[1], tile):
                total[:, lower : lower + tile] += jnp.dot(
                    held[g],
                    weights[g, :, lower : lower + tile],
                    preferred_element_type=jnp.float32,
                )

        return carry

    lax.fori_loop(0, CHUNKS + 1, step, 0)
    out_ref[...] = total[...].astype(jnp.bfloat16)

    def finish(f, carry):
        gather.wait_sends(f)
        return carry

    lax.fori_loop(0, CHUNKS, finish, 0)


def project(n_tp, rows_here, gain, w_query, w_key, w_value):
    rows, model_width = rows_here.shape
    width = model_width // CHUNKS
    columns = w_query.shape[1] + w_key.shape[1] + w_value.shape[1]
    vmem, hbm = pl.BlockSpec(memory_space=pltpu.VMEM), pl.BlockSpec(memory_space=pl.ANY)
    return pl.pallas_call(
        functools.partial(project_kernel, n_tp),
        out_shape=jax.ShapeDtypeStruct((n_tp * rows, columns), jnp.bfloat16),
        in_specs=[vmem, vmem, hbm, hbm, hbm],
        out_specs=vmem,
        scratch_shapes=gather_scratch(n_tp, rows, width)
        + [
            pltpu.VMEM((CHUNKS, width, columns), jnp.bfloat16),
            pltpu.VMEM((n_tp * rows, columns), jnp.float32),
            pltpu.SemaphoreType.DMA((CHUNKS, 3)),
        ],
        compiler_params=pltpu.CompilerParams(
            collective_id=0, has_side_effects=True, vmem_limit_bytes=VMEM_BYTES
        ),
        name="gather_project",
    )(rows_here, gain.reshape(1, model_width), w_query, w_key, w_value)


def talk_kernel(
    n_tp, n_grp, attended_ref, wo_ref, x_ref, gain_ref, wt_ref, routing_ref, out_ref,
    held, sib_send, chip_send, pass_send, recv,
    ordered, w_out, w_talk, kept, pair_out, pair_in, chip_out, chip_in,
    total, square_sum, owner_out, owner_in,
    wo_sem, wt_sem, pair_send, pair_recv, part_send, part_recv, owner_send, owner_recv,
):
    width = held.shape[2]
    model_width = width * CHUNKS
    head_width = GQA * HEAD_DIM

    def weight_copies(f):
        start = pl.multiple_of(f * width, width)
        return (
            pltpu.make_async_copy(wo_ref.at[:, pl.ds(start, width)], w_out.at[f], wo_sem.at[f]),
            pltpu.make_async_copy(wt_ref.at[pl.ds(start, width), :], w_talk.at[f], wt_sem.at[f]),
        )

    def start_weights(which):
        def body(f, carry):
            weight_copies(f)[which].start()
            return carry

        lax.fori_loop(0, CHUNKS, body, 0)

    start_weights(0)
    start_weights(1)
    gather = RowGather(n_tp, held, sib_send, chip_send, pass_send, recv)
    me, chip, core, sibling = gather.me, gather.chip, gather.core, gather.sibling
    n_chips, rows = gather.n_chips, gather.rows
    half = n_chips * rows
    for c in range(n_chips):
        for side, owner in enumerate((2 * c + 1 - core, 2 * c + core)):
            ordered[side * half + c * rows : side * half + (c + 1) * rows, :] = attended_ref[
                pl.ds(pl.multiple_of(owner * rows, rows), rows), :
            ]
    greet(n_tp, n_grp)

    def pair_copy(f):
        return remote(
            pair_out.at[f], pair_in.at[f], pair_send.at[f], pair_recv.at[f], {"tp": sibling}
        )

    def part_copy(f, j):
        return remote(
            chip_out.at[f, j - 1],
            chip_in.at[f, j - 1],
            part_send.at[f, j - 1],
            part_recv.at[f, j - 1],
            {"tp": gather.partner(j)},
        )

    tile = column_tile(width)

    def reduce_step(f, carry):
        @pl.when(f < CHUNKS)
        def _():
            weight_copies(f)[0].wait()
            for lower in range(0, width, tile):
                summed = None
                for first in range(0, ordered.shape[1], head_width):
                    part = jnp.dot(
                        ordered[:, first : first + head_width],
                        w_out[f, first : first + head_width, lower : lower + tile],
                        preferred_element_type=jnp.float32,
                    )
                    part = part.astype(jnp.bfloat16).astype(jnp.float32)
                    summed = part if summed is None else summed + part
                pair_out[f, :, lower : lower + tile] = summed[:half].astype(jnp.bfloat16)
                kept[f, :, lower : lower + tile] = summed[half:]
            pair_copy(f).start()

        @pl.when(f >= 1)
        def _():
            g = f - 1
            pair_copy(g).wait_recv()
            for j in range(1, n_chips):
                there = pl.ds(pl.multiple_of(lax.rem(chip + j, n_chips) * rows, rows), rows)
                both = kept[g, there, :] + pair_in[g, there, :].astype(jnp.float32)
                chip_out[g, j - 1] = both.astype(jnp.bfloat16)
                part_copy(g, j).start()

        return carry

    lax.fori_loop(0, CHUNKS + 1, reduce_step, 0)

    def hidden_step(f, carry):
        here = pl.ds(pl.multiple_of(chip * rows, rows), rows)
        both = kept[f, here, :] + pair_in[f, here, :].astype(jnp.float32)
        for j in range(1, n_chips):
            part_copy(f, j).wait_recv()
            both = both + chip_in[f, j - 1].astype(jnp.float32)
        columns = pl.ds(pl.multiple_of(f * width, width), width)
        hidden = x_ref[:, columns].astype(jnp.float32) + both
        held[f, pl.ds(pl.multiple_of(me * rows, rows), rows), :] = hidden.astype(jnp.bfloat16)
        gather.send(f)
        return carry

    lax.fori_loop(0, CHUNKS, hidden_step, 0)
    total[...] = jnp.zeros_like(total)
    square_sum[...] = jnp.zeros_like(square_sum)

    def talk_step(f, carry):
        @pl.when(f < CHUNKS)
        def _():
            gather.pass_on(f)

        @pl.when(f >= 1)
        def _():
            g = f - 1
            gather.wait_sibling(g)
            weight_copies(g)[1].wait()
            hidden = held[g].astype(jnp.float32)
            square_sum[...] += jnp.sum(hidden * hidden, axis=1, keepdims=True)
            columns = pl.ds(pl.multiple_of(g * width, width), width)
            gained = (hidden * gain_ref[:, columns].astype(jnp.float32)).astype(jnp.bfloat16)
            total[...] += jnp.dot(gained, w_talk[g], preferred_element_type=jnp.float32)

        return carry

    lax.fori_loop(0, CHUNKS + 1, talk_step, 0)
    scale = lax.rsqrt(square_sum[...] / model_width + EPSILON)
    talk = (total[...] * scale).astype(jnp.bfloat16)
    pitch = owner_out.shape[1]
    grp = lax.axis_index("grp")

    def owner_copy(j):
        target = lax.rem(grp + j, n_grp)
        return remote(
            owner_out.at[target],
            owner_in.at[j],
            owner_send.at[j],
            owner_recv.at[j],
            {"grp": target},
        )

    routed = jnp.dot(routing_ref[...], talk, preferred_element_type=jnp.float32)
    for o in range(n_grp):
        owner_out[o] = routed[o * pitch : (o + 1) * pitch].astype(jnp.bfloat16)
    for j in range(1, n_grp):
        owner_copy(j).start()
    out_ref[grp] = owner_out[grp]
    for j in range(1, n_grp):
        owner_copy(j).wait_recv()
        out_ref[lax.rem(grp + n_grp - j, n_grp)] = owner_in[j]

    def finish(f, carry):
        gather.wait_sends(f)
        pair_copy(f).wait_send()
        for j in range(1, n_chips):
            part_copy(f, j).wait_send()
        return carry

    lax.fori_loop(0, CHUNKS, finish, 0)
    for j in range(1, n_grp):
        owner_copy(j).wait_send()


def talk(n_tp, n_grp, attended, w_out, rows_here, gain, w_talker, routing):
    rows, model_width = rows_here.shape
    width = model_width // CHUNKS
    columns = w_talker.shape[1]
    other = max(1, n_tp // 2 - 1)
    half = n_tp // 2 * rows
    pitch = routing.shape[0] // n_grp
    vmem, hbm = pl.BlockSpec(memory_space=pltpu.VMEM), pl.BlockSpec(memory_space=pl.ANY)
    bf16, dma = jnp.bfloat16, pltpu.SemaphoreType.DMA
    return pl.pallas_call(
        functools.partial(talk_kernel, n_tp, n_grp),
        out_shape=jax.ShapeDtypeStruct((n_grp, pitch, columns), bf16),
        in_specs=[vmem, hbm, vmem, vmem, hbm, vmem],
        out_specs=vmem,
        scratch_shapes=gather_scratch(n_tp, rows, width)
        + [
            pltpu.VMEM(attended.shape, bf16),
            pltpu.VMEM((CHUNKS, w_out.shape[0], width), bf16),
            pltpu.VMEM((CHUNKS, width, columns), bf16),
            pltpu.VMEM((CHUNKS, half, width), jnp.float32),
            pltpu.VMEM((CHUNKS, half, width), bf16),
            pltpu.VMEM((CHUNKS, half, width), bf16),
            pltpu.VMEM((CHUNKS, other, rows, width), bf16),
            pltpu.VMEM((CHUNKS, other, rows, width), bf16),
            pltpu.VMEM((n_tp * rows, columns), jnp.float32),
            pltpu.VMEM((n_tp * rows, 1), jnp.float32),
            pltpu.VMEM((n_grp, pitch, columns), bf16),
            pltpu.VMEM((n_grp, pitch, columns), bf16),
            dma((CHUNKS,)),
            dma((CHUNKS,)),
            dma((CHUNKS,)),
            dma((CHUNKS,)),
            dma((CHUNKS, other)),
            dma((CHUNKS, other)),
            dma((n_grp,)),
            dma((n_grp,)),
        ],
        compiler_params=pltpu.CompilerParams(
            collective_id=1, has_side_effects=True, vmem_limit_bytes=VMEM_BYTES
        ),
        name="reduce_talk",
    )(attended, w_out, rows_here, gain.reshape(1, model_width), w_talker, routing)


def slot_tables(session_row, owner_row):
    session_range = jnp.arange(SESS, dtype=jnp.int32)
    member = (session_row[:, None] == session_range[None, :]).astype(jnp.int32)
    counts = jnp.sum(member, axis=0)
    starts = jnp.cumsum(counts) - counts
    first_row = jnp.sum(member * starts[None, :], axis=1)
    position = jnp.arange(session_row.shape[0], dtype=jnp.int32) - first_row
    earlier = (owner_row[:, None] == owner_row[None, :]) & (
        session_range[None, :] < session_range[:, None]
    )
    owner_rank = jnp.sum(earlier.astype(jnp.int32), axis=1)
    owner_slot = owner_row * OWNER_PITCH + owner_rank * MOST
    destination = jnp.sum(member * owner_slot[None, :], axis=1) + position
    return (counts, position, destination)


def attend(q_slots, k_slots, v_slots, cache_k, cache_v, live_lens, counts):
    score_scale = HEAD_DIM ** (-0.5)
    cached = (
        jnp.einsum("smkgd,sckd->skgmc", q_slots, cache_k, preferred_element_type=jnp.float32)
        * score_scale
    )
    fresh = (
        jnp.einsum("smkgd,snkd->skgmn", q_slots, k_slots, preferred_element_type=jnp.float32)
        * score_scale
    )
    live_cache = jnp.arange(cache_k.shape[1], dtype=jnp.int32)[None, :] < live_lens[:, None]
    places = jnp.arange(MOST, dtype=jnp.int32)
    causal = places[None, :] <= places[:, None]
    live_fresh = causal[None, :, :] & (places[None, None, :] < counts[:, None, None])
    cached = jnp.where(live_cache[:, None, None, None, :], cached, -1e30)
    fresh = jnp.where(live_fresh[:, None, None, :, :], fresh, -1e30)
    highest = jnp.maximum(jnp.max(cached, axis=-1), jnp.max(fresh, axis=-1))
    exp_cached = jnp.exp(cached - highest[..., None])
    exp_fresh = jnp.exp(fresh - highest[..., None])
    denominator = jnp.sum(exp_cached, axis=-1) + jnp.sum(exp_fresh, axis=-1)
    weight_cached = (exp_cached / denominator[..., None]).astype(jnp.bfloat16)
    weight_fresh = (exp_fresh / denominator[..., None]).astype(jnp.bfloat16)
    mixed = jnp.einsum(
        "skgmc,sckd->smkgd", weight_cached, cache_v, preferred_element_type=jnp.float32
    )
    mixed = mixed + jnp.einsum(
        "skgmn,snkd->smkgd", weight_fresh, v_slots, preferred_element_type=jnp.float32
    )
    return mixed.astype(jnp.bfloat16)


def on_device(
    thinker_rows,
    norm_gain,
    w_query,
    w_key,
    w_value,
    w_out,
    cache_keys,
    cache_values,
    session_ids,
    cache_lens,
    owners,
    talker_gain,
    w_talker,
):
    n_tp, n_grp = lax.axis_size("tp"), lax.axis_size("grp")
    kv_local = w_key.shape[1] // HEAD_DIM
    head_width = GQA * HEAD_DIM
    slot_count = SESS * MOST
    qkv = project(n_tp, thinker_rows, norm_gain, w_query, w_key, w_value)
    counts, position, destination = slot_tables(session_ids[0], owners[:, 0])
    slot_index = session_ids[0] * MOST + position
    placing = (slot_index[None, :] == jnp.arange(slot_count, dtype=jnp.int32)[:, None]).astype(
        jnp.bfloat16
    )
    slots = jnp.dot(placing, qkv, preferred_element_type=jnp.float32).astype(jnp.bfloat16)
    q_slots, k_slots, v_slots = jnp.split(
        slots, [w_query.shape[1], w_query.shape[1] + w_key.shape[1]], axis=1
    )
    mixed = attend(
        q_slots.reshape(SESS, MOST, kv_local, GQA, HEAD_DIM),
        k_slots.reshape(SESS, MOST, kv_local, HEAD_DIM),
        v_slots.reshape(SESS, MOST, kv_local, HEAD_DIM),
        cache_keys.reshape(SESS, cache_keys.shape[1], kv_local, HEAD_DIM),
        cache_values.reshape(SESS, cache_values.shape[1], kv_local, HEAD_DIM),
        cache_lens[0],
        counts,
    )
    attended = lax.dot_general(
        placing,
        mixed.reshape(slot_count, kv_local * head_width),
        (((0,), (0,)), ((), ())),
        preferred_element_type=jnp.float32,
    ).astype(jnp.bfloat16)
    routing = (
        destination[None, :] == jnp.arange(n_grp * OWNER_PITCH, dtype=jnp.int32)[:, None]
    ).astype(jnp.bfloat16)
    placed = talk(n_tp, n_grp, attended, w_out, thinker_rows, talker_gain, w_talker, routing)
    return placed[:, : CAPS * MOST].reshape(n_grp * CAPS * MOST, w_talker.shape[1])


def solution(mesh):
    return jax.shard_map(
        on_device,
        mesh=mesh,
        in_specs=(
            P(("grp", "tp"), None),
            P(),
            P(None, "tp"),
            P(None, "tp"),
            P(None, "tp"),
            P("tp", None),
            P("grp", None, "tp"),
            P("grp", None, "tp"),
            P("grp", None),
            P("grp", None),
            P("grp", None),
            P(),
            P(None, "tp"),
        ),
        out_specs=P("grp", "tp"),
        check_vma=False,
    )
```

```python
import functools

import jax
import jax.numpy as jnp
from jax import lax
from jax.experimental import pallas as pl
from jax.experimental.pallas import tpu as pltpu
from jax.sharding import PartitionSpec as P

HEAD_DIM = 128
SESS = 16
CAPS = 2
GQA = 4
MOST = 20
OWNER_PITCH = 48
SLOT_PITCH = 24
CHUNKS = 8
VMEM_BYTES = 58 * 1024 * 1024

EPSILON = 1e-06
MESH = pl.DeviceIdType.MESH


def places(n_tp):
    me = lax.axis_index("tp")
    core = lax.rem(me, 2)
    chip = me // 2
    return me, chip, core, me + 1 - 2 * core


def greet(n_tp, n_grp=1):
    me, chip, core, sibling = places(n_tp)
    n_chips = n_tp // 2
    barrier = pltpu.get_barrier_semaphore()
    peers = [{"tp": sibling}]
    for j in range(1, n_chips):
        peers.append({"tp": lax.rem(chip + j, n_chips) * 2 + core})
    grp = lax.axis_index("grp")
    for j in range(1, n_grp):
        peers.append({"grp": lax.rem(grp + j, n_grp)})
    for peer in peers:
        pl.semaphore_signal(barrier, inc=1, device_id=peer, device_id_type=MESH)
    return functools.partial(pl.semaphore_wait, barrier, len(peers))


def remote(src, dst, send, recv, device):
    return pltpu.make_async_remote_copy(
        src_ref=src,
        dst_ref=dst,
        send_sem=send,
        recv_sem=recv,
        device_id=device,
        device_id_type=MESH,
    )


class RowGather:
    def __init__(self, n_tp, held, sib_send, chip_send, pass_send, recv):
        self.held, self.recv = held, recv
        self.sib_send, self.chip_send, self.pass_send = sib_send, chip_send, pass_send
        self.me, self.chip, self.core, self.sibling = places(n_tp)
        self.n_chips = n_tp // 2
        self.rows = held.shape[1] // n_tp

    def block(self, f, owner):
        start = pl.multiple_of(owner * self.rows, self.rows)
        return self.held.at[f, pl.ds(start, self.rows), :]

    def copy(self, f, owner, send, target):
        ref = self.block(f, owner)
        return remote(ref, ref, send, self.recv.at[f, owner], {"tp": target})

    def partner(self, j):
        return lax.rem(self.chip + j, self.n_chips) * 2 + self.core

    def own_copies(self, f):
        copies = [
            self.copy(f, self.me, self.chip_send.at[f, j - 1], self.partner(j))
            for j in range(1, self.n_chips)
        ]
        return copies + [self.copy(f, self.me, self.sib_send.at[f], self.sibling)]

    def passed_copies(self, f):
        return [
            self.copy(f, self.partner(j), self.pass_send.at[f, j - 1], self.sibling)
            for j in range(1, self.n_chips)
        ]

    def send(self, f):
        for copy in self.own_copies(f):
            copy.start()

    def pass_on(self, f):
        for copy in self.passed_copies(f):
            copy.wait_recv()
            copy.start()

    def wait_sibling(self, f):
        self.copy(f, self.sibling, self.sib_send.at[f], self.sibling).wait_recv()
        for j in range(1, self.n_chips):
            owner = lax.rem(self.chip + j, self.n_chips) * 2 + 1 - self.core
            self.copy(f, owner, self.pass_send.at[f, j - 1], self.sibling).wait_recv()

    def wait_sends(self, f):
        for copy in self.own_copies(f) + self.passed_copies(f):
            copy.wait_send()


def gather_scratch(n_tp, rows, width):
    other = max(1, n_tp // 2 - 1)
    return [
        pltpu.VMEM((CHUNKS, n_tp * rows, width), jnp.bfloat16),
        pltpu.SemaphoreType.DMA((CHUNKS,)),
        pltpu.SemaphoreType.DMA((CHUNKS, other)),
        pltpu.SemaphoreType.DMA((CHUNKS, other)),
        pltpu.SemaphoreType.DMA((CHUNKS, n_tp)),
    ]


def column_tile(columns):
    return 512 if columns % 512 == 0 else 256 if columns % 256 == 0 else 128


def project_kernel(
    n_tp, x_ref, gain_ref, wq_ref, wk_ref, wv_ref, out_ref,
    held, sib_send, chip_send, pass_send, recv, weights, total, w_sem,
):
    width = held.shape[2]
    model_width = width * CHUNKS
    edges = [0]
    for ref in (wq_ref, wk_ref, wv_ref):
        edges.append(edges[-1] + ref.shape[1])

    def weight_copies(f):
        start = pl.multiple_of(f * width, width)
        return [
            pltpu.make_async_copy(
                ref.at[pl.ds(start, width), :],
                weights.at[f, :, pl.ds(edges[i], ref.shape[1])],
                w_sem.at[f, i],
            )
            for i, ref in enumerate((wq_ref, wk_ref, wv_ref))
        ]

    def start_weights(f, carry):
        for copy in weight_copies(f):
            copy.start()
        return carry

    greeted = greet(n_tp)
    lax.fori_loop(0, CHUNKS, start_weights, 0)
    gather = RowGather(n_tp, held, sib_send, chip_send, pass_send, recv)

    def squares(f, carry):
        part = x_ref[:, pl.ds(pl.multiple_of(f * width, width), width)].astype(jnp.float32)
        return carry + jnp.sum(part * part, axis=1, keepdims=True)

    square_sum = lax.fori_loop(
        0, CHUNKS, squares, jnp.zeros((x_ref.shape[0], 1), jnp.float32)
    )
    scale = lax.rsqrt(square_sum / model_width + EPSILON)
    rows = gather.rows
    greeted()

    def normalise(f, carry):
        columns = pl.ds(pl.multiple_of(f * width, width), width)
        part = x_ref[:, columns].astype(jnp.float32) * scale
        part = part * gain_ref[columns][None, :].astype(jnp.float32)
        start = pl.multiple_of(gather.me * rows, rows)
        held[f, pl.ds(start, rows), :] = part.astype(jnp.bfloat16)
        gather.send(f)
        return carry

    lax.fori_loop(0, CHUNKS, normalise, 0)
    total[...] = jnp.zeros_like(total)
    tile = column_tile(total.shape[1])

    def step(f, carry):
        @pl.when(f < CHUNKS)
        def _():
            gather.pass_on(f)

        @pl.when(f >= 1)
        def _():
            g = f - 1
            gather.wait_sibling(g)
            for copy in weight_copies(g):
                copy.wait()
            for lower in range(0, total.shape[1], tile):
                total[:, lower : lower + tile] += jnp.dot(
                    held[g],
                    weights[g, :, lower : lower + tile],
                    preferred_element_type=jnp.float32,
                )

        return carry

    lax.fori_loop(0, CHUNKS + 1, step, 0)
    out_ref[...] = total[...].astype(jnp.bfloat16)

    def finish(f, carry):
        gather.wait_sends(f)
        return carry

    lax.fori_loop(0, CHUNKS, finish, 0)


def project(n_tp, rows_here, gain, w_query, w_key, w_value):
    rows, model_width = rows_here.shape
    width = model_width // CHUNKS
    columns = w_query.shape[1] + w_key.shape[1] + w_value.shape[1]
    vmem, hbm = pl.BlockSpec(memory_space=pltpu.VMEM), pl.BlockSpec(memory_space=pl.ANY)
    return pl.pallas_call(
        functools.partial(project_kernel, n_tp),
        out_shape=jax.ShapeDtypeStruct((n_tp * rows, columns), jnp.bfloat16),
        in_specs=[vmem, vmem, hbm, hbm, hbm],
        out_specs=vmem,
        scratch_shapes=gather_scratch(n_tp, rows, width)
        + [
            pltpu.VMEM((CHUNKS, width, columns), jnp.bfloat16),
            pltpu.VMEM((n_tp * rows, columns), jnp.float32),
            pltpu.SemaphoreType.DMA((CHUNKS, 3)),
        ],
        compiler_params=pltpu.CompilerParams(
            collective_id=0, has_side_effects=True, vmem_limit_bytes=VMEM_BYTES
        ),
        name="gather_project",
    )(rows_here, gain, w_query, w_key, w_value)


def slot_tables(ids_ref, owners_ref):
    ids = ids_ref[...]
    tokens = ids.shape[1]
    session = lax.broadcasted_iota(jnp.int32, (SESS, tokens), 0)
    member = (ids == session).astype(jnp.int32)
    starts = jnp.sum((ids < session).astype(jnp.int32), axis=1, keepdims=True)
    first = jnp.sum(member * starts, axis=0, keepdims=True)
    position = lax.broadcasted_iota(jnp.int32, (1, tokens), 1) - first
    one = lax.broadcasted_iota(jnp.int32, (SESS, SESS), 0)
    two = lax.broadcasted_iota(jnp.int32, (SESS, SESS), 1)
    named = owners_ref[...]
    owner = jnp.sum(jnp.where(one == two, named, 0), axis=1, keepdims=True)
    earlier = (owner == named) & (two < one)
    rank = jnp.sum(earlier.astype(jnp.int32), axis=1, keepdims=True)
    owner_slot = owner * OWNER_PITCH + rank * MOST
    destination = jnp.sum(member * owner_slot, axis=0, keepdims=True) + position
    return ids * SLOT_PITCH + position, destination


def attend(slot, qkv_ref, cache_copies, keys, values, lens_ref, slots, mixed, attended_ref):
    score_scale = HEAD_DIM ** (-0.5)
    n_cache = keys.shape[1]
    kv_local = keys.shape[2] // HEAD_DIM
    q_width = kv_local * GQA * HEAD_DIM
    kv_width = kv_local * HEAD_DIM
    slot_count = SESS * SLOT_PITCH
    slot_rows = lax.broadcasted_iota(jnp.int32, (slot_count, slot.shape[1]), 0)
    placing = (slot_rows == slot).astype(jnp.float32)
    tile = column_tile(slots.shape[1])
    for lower in range(0, slots.shape[1], tile):
        slots[:, lower : lower + tile] = jnp.dot(
            placing.astype(jnp.bfloat16),
            qkv_ref[:, lower : lower + tile],
            preferred_element_type=jnp.float32,
        )
    many = GQA * SLOT_PITCH
    cache_place = lax.broadcasted_iota(jnp.int32, (many, n_cache), 1)
    row = lax.broadcasted_iota(jnp.int32, (GQA, SLOT_PITCH, SLOT_PITCH), 1)
    column = lax.broadcasted_iota(jnp.int32, (GQA, SLOT_PITCH, SLOT_PITCH), 2)
    row, column = row.reshape(many, SLOT_PITCH), column.reshape(many, SLOT_PITCH)
    transposed = (((1,), (1,)), ((), ()))

    def one_session(s):
        for copy in cache_copies(s):
            copy.wait()
        rows = pl.ds(pl.multiple_of(s * SLOT_PITCH, 8), SLOT_PITCH)
        live = cache_place < lens_ref[0, s]
        for k in range(kv_local):
            heads = [
                slots[rows, pl.ds((k * GQA + g) * HEAD_DIM, HEAD_DIM)] for g in range(GQA)
            ]
            query = jnp.concatenate(heads, axis=0).astype(jnp.bfloat16)
            lower = q_width + k * HEAD_DIM
            key_new = slots[rows, pl.ds(lower, HEAD_DIM)].astype(jnp.bfloat16)
            value_new = slots[rows, pl.ds(lower + kv_width, HEAD_DIM)].astype(jnp.bfloat16)
            here = pl.ds(k * HEAD_DIM, HEAD_DIM)
            cached = lax.dot_general(
                query, keys[s, :, here], transposed, preferred_element_type=jnp.float32
            )
            fresh = lax.dot_general(
                query, key_new, transposed, preferred_element_type=jnp.float32
            )
            cached = jnp.where(live, cached * score_scale, -1e30)
            fresh = jnp.where(column <= row, fresh * score_scale, -1e30)
            highest = jnp.maximum(
                jnp.max(cached, axis=1, keepdims=True), jnp.max(fresh, axis=1, keepdims=True)
            )
            cached = jnp.exp(cached - highest)
            fresh = jnp.exp(fresh - highest)
            inverse = 1.0 / (
                jnp.sum(cached, axis=1, keepdims=True) + jnp.sum(fresh, axis=1, keepdims=True)
            )
            sums = jnp.dot(
                (cached * inverse).astype(jnp.bfloat16),
                values[s, :, here],
                preferred_element_type=jnp.float32,
            ) + jnp.dot(
                (fresh * inverse).astype(jnp.bfloat16),
                value_new,
                preferred_element_type=jnp.float32,
            )
            for g in range(GQA):
                mixed[rows, pl.ds((k * GQA + g) * HEAD_DIM, HEAD_DIM)] = sums[
                    g * SLOT_PITCH : (g + 1) * SLOT_PITCH
                ]

    def sessions(i, carry):
        one_session(2 * i)
        one_session(2 * i + 1)
        return carry

    lax.fori_loop(0, SESS // 2, sessions, 0)
    back = placing.T.astype(jnp.bfloat16)
    tile = column_tile(q_width)
    for lower in range(0, q_width, tile):
        attended_ref[:, lower : lower + tile] = jnp.dot(
            back,
            mixed[:, lower : lower + tile].astype(jnp.bfloat16),
            preferred_element_type=jnp.float32,
        ).astype(jnp.bfloat16)


def talk_kernel(
    n_tp, n_grp, qkv_ref, ck_ref, cv_ref, ids_ref, lens_ref, owners_ref,
    wo_ref, x_ref, gain_ref, wt_ref, out_ref,
    held, sib_send, chip_send, pass_send, recv,
    ordered, w_out, w_talk, kept, pair_out, pair_in, chip_out, chip_in,
    total, square_sum, owner_out, owner_in,
    keys, values, slots, mixed, attended_ref, cache_sem, wo_sem, wt_sem, pair_send, pair_recv, part_send, part_recv, owner_send, owner_recv,
):
    width = held.shape[2]
    model_width = width * CHUNKS
    head_width = GQA * HEAD_DIM

    def weight_copies(f):
        start = pl.multiple_of(f * width, width)
        return (
            pltpu.make_async_copy(wo_ref.at[:, pl.ds(start, width)], w_out.at[f], wo_sem.at[f]),
            pltpu.make_async_copy(wt_ref.at[pl.ds(start, width), :], w_talk.at[f], wt_sem.at[f]),
        )

    def start_weights(which):
        def body(f, carry):
            weight_copies(f)[which].start()
            return carry

        lax.fori_loop(0, CHUNKS, body, 0)

    def cache_copies(s):
        return (
            pltpu.make_async_copy(ck_ref.at[s], keys.at[s], cache_sem.at[s, 0]),
            pltpu.make_async_copy(cv_ref.at[s], values.at[s], cache_sem.at[s, 1]),
        )

    def start_cache(s, carry):
        for copy in cache_copies(s):
            copy.start()
        return carry

    greeted = greet(n_tp, n_grp)
    lax.fori_loop(0, SESS, start_cache, 0)
    start_weights(0)
    start_weights(1)
    slot, destination = slot_tables(ids_ref, owners_ref)
    attend(slot, qkv_ref, cache_copies, keys, values, lens_ref, slots, mixed, attended_ref)
    gather = RowGather(n_tp, held, sib_send, chip_send, pass_send, recv)
    me, chip, core, sibling = gather.me, gather.chip, gather.core, gather.sibling
    n_chips, rows = gather.n_chips, gather.rows
    half = n_chips * rows
    for c in range(n_chips):
        for side, owner in enumerate((2 * c + 1 - core, 2 * c + core)):
            ordered[side * half + c * rows : side * half + (c + 1) * rows, :] = attended_ref[
                pl.ds(pl.multiple_of(owner * rows, rows), rows), :
            ]
    greeted()

    def pair_copy(f):
        return remote(
            pair_out.at[f], pair_in.at[f], pair_send.at[f], pair_recv.at[f], {"tp": sibling}
        )

    def part_copy(f, j):
        return remote(
            chip_out.at[f, j - 1],
            chip_in.at[f, j - 1],
            part_send.at[f, j - 1],
            part_recv.at[f, j - 1],
            {"tp": gather.partner(j)},
        )

    tile = column_tile(width)

    def reduce_step(f, carry):
        @pl.when(f < CHUNKS)
        def _():
            weight_copies(f)[0].wait()
            for lower in range(0, width, tile):
                summed = None
                for first in range(0, ordered.shape[1], head_width):
                    part = jnp.dot(
                        ordered[:, first : first + head_width],
                        w_out[f, first : first + head_width, lower : lower + tile],
                        preferred_element_type=jnp.float32,
                    )
                    part = part.astype(jnp.bfloat16).astype(jnp.float32)
                    summed = part if summed is None else summed + part
                pair_out[f, :, lower : lower + tile] = summed[:half].astype(jnp.bfloat16)
                kept[f, :, lower : lower + tile] = summed[half:]
            pair_copy(f).start()

        @pl.when(f >= 1)
        def _():
            g = f - 1
            pair_copy(g).wait_recv()
            for j in range(1, n_chips):
                there = pl.ds(pl.multiple_of(lax.rem(chip + j, n_chips) * rows, rows), rows)
                both = kept[g, there, :] + pair_in[g, there, :].astype(jnp.float32)
                chip_out[g, j - 1] = both.astype(jnp.bfloat16)
                part_copy(g, j).start()

        return carry

    lax.fori_loop(0, CHUNKS + 1, reduce_step, 0)

    def hidden_step(f, carry):
        here = pl.ds(pl.multiple_of(chip * rows, rows), rows)
        both = kept[f, here, :] + pair_in[f, here, :].astype(jnp.float32)
        for j in range(1, n_chips):
            part_copy(f, j).wait_recv()
            both = both + chip_in[f, j - 1].astype(jnp.float32)
        columns = pl.ds(pl.multiple_of(f * width, width), width)
        hidden = x_ref[:, columns].astype(jnp.float32) + both
        held[f, pl.ds(pl.multiple_of(me * rows, rows), rows), :] = hidden.astype(jnp.bfloat16)
        gather.send(f)
        return carry

    lax.fori_loop(0, CHUNKS, hidden_step, 0)
    total[...] = jnp.zeros_like(total)
    square_sum[...] = jnp.zeros_like(square_sum)

    def talk_step(f, carry):
        @pl.when(f < CHUNKS)
        def _():
            gather.pass_on(f)

        @pl.when(f >= 1)
        def _():
            g = f - 1
            gather.wait_sibling(g)
            weight_copies(g)[1].wait()
            hidden = held[g].astype(jnp.float32)
            square_sum[...] += jnp.sum(hidden * hidden, axis=1, keepdims=True)
            columns = pl.ds(pl.multiple_of(g * width, width), width)
            gained = (hidden * gain_ref[columns][None, :].astype(jnp.float32)).astype(jnp.bfloat16)
            total[...] += jnp.dot(gained, w_talk[g], preferred_element_type=jnp.float32)

        return carry

    lax.fori_loop(0, CHUNKS + 1, talk_step, 0)
    scale = lax.rsqrt(square_sum[...] / model_width + EPSILON)
    talk = (total[...] * scale).astype(jnp.bfloat16)
    pitch = owner_out.shape[1]
    grp = lax.axis_index("grp")

    def owner_copy(j):
        target = lax.rem(grp + j, n_grp)
        return remote(
            owner_out.at[target],
            owner_in.at[grp],
            owner_send.at[j],
            owner_recv.at[grp],
            {"grp": target},
        )

    def owner_arrival(j):
        source = lax.rem(grp + n_grp - j, n_grp)
        return remote(
            owner_out.at[source],
            owner_in.at[source],
            owner_send.at[j],
            owner_recv.at[source],
            {"grp": source},
        )

    routing_rows = lax.broadcasted_iota(jnp.int32, (n_grp * pitch, talk.shape[0]), 0)
    routing = (routing_rows == destination).astype(jnp.float32).astype(jnp.bfloat16)
    routed = jnp.dot(routing, talk, preferred_element_type=jnp.float32)
    for o in range(n_grp):
        owner_out[o] = routed[o * pitch : (o + 1) * pitch].astype(jnp.bfloat16)
    for j in range(1, n_grp):
        owner_copy(j).start()
    owner_in[grp] = owner_out[grp]
    for j in range(1, n_grp):
        owner_arrival(j).wait_recv()
    used = CAPS * MOST
    out_ref[...] = jnp.concatenate(
        [owner_in[o].astype(jnp.float32)[:used] for o in range(n_grp)], axis=0
    ).astype(jnp.bfloat16)

    def finish(f, carry):
        gather.wait_sends(f)
        pair_copy(f).wait_send()
        for j in range(1, n_chips):
            part_copy(f, j).wait_send()
        return carry

    lax.fori_loop(0, CHUNKS, finish, 0)
    for j in range(1, n_grp):
        owner_copy(j).wait_send()


def talk(
    n_tp, n_grp, qkv, cache_keys, cache_values, session_ids, cache_lens, owners,
    w_out, rows_here, gain, w_talker,
):
    rows, model_width = rows_here.shape
    width = model_width // CHUNKS
    columns = w_talker.shape[1]
    other = max(1, n_tp // 2 - 1)
    half = n_tp // 2 * rows
    pitch = OWNER_PITCH
    slot_count = SESS * SLOT_PITCH
    q_width = w_out.shape[0]
    vmem, hbm = pl.BlockSpec(memory_space=pltpu.VMEM), pl.BlockSpec(memory_space=pl.ANY)
    smem = pl.BlockSpec(memory_space=pltpu.SMEM)
    bf16, dma = jnp.bfloat16, pltpu.SemaphoreType.DMA
    return pl.pallas_call(
        functools.partial(talk_kernel, n_tp, n_grp),
        out_shape=jax.ShapeDtypeStruct((n_grp * CAPS * MOST, columns), bf16),
        in_specs=[vmem, hbm, hbm, vmem, smem, vmem, hbm, vmem, vmem, hbm],
        out_specs=vmem,
        scratch_shapes=gather_scratch(n_tp, rows, width)
        + [
            pltpu.VMEM((n_tp * rows, q_width), bf16),
            pltpu.VMEM((CHUNKS, w_out.shape[0], width), bf16),
            pltpu.VMEM((CHUNKS, width, columns), bf16),
            pltpu.VMEM((CHUNKS, half, width), jnp.float32),
            pltpu.VMEM((CHUNKS, half, width), bf16),
            pltpu.VMEM((CHUNKS, half, width), bf16),
            pltpu.VMEM((CHUNKS, other, rows, width), bf16),
            pltpu.VMEM((CHUNKS, other, rows, width), bf16),
            pltpu.VMEM((n_tp * rows, columns), jnp.float32),
            pltpu.VMEM((n_tp * rows, 1), jnp.float32),
            pltpu.VMEM((n_grp, pitch, columns), bf16),
            pltpu.VMEM((n_grp, pitch, columns), bf16),
            pltpu.VMEM(cache_keys.shape, bf16),
            pltpu.VMEM(cache_values.shape, bf16),
            pltpu.VMEM((slot_count, qkv.shape[1]), jnp.float32),
            pltpu.VMEM((slot_count, q_width), jnp.float32),
            pltpu.VMEM((n_tp * rows, q_width), bf16),
            dma((SESS, 2)),
            dma((CHUNKS,)),
            dma((CHUNKS,)),
            dma((CHUNKS,)),
            dma((CHUNKS,)),
            dma((CHUNKS, other)),
            dma((CHUNKS, other)),
            dma((n_grp,)),
            dma((n_grp,)),
        ],
        compiler_params=pltpu.CompilerParams(
            collective_id=1, has_side_effects=True, vmem_limit_bytes=VMEM_BYTES
        ),
        name="attend_talk",
    )(
        qkv, cache_keys, cache_values, session_ids, cache_lens, owners.reshape(1, SESS),
        w_out, rows_here, gain, w_talker,
    )


def on_device(
    thinker_rows,
    norm_gain,
    w_query,
    w_key,
    w_value,
    w_out,
    cache_keys,
    cache_values,
    session_ids,
    cache_lens,
    owners,
    talker_gain,
    w_talker,
):
    n_tp, n_grp = lax.axis_size("tp"), lax.axis_size("grp")
    qkv = project(n_tp, thinker_rows, norm_gain, w_query, w_key, w_value)
    return talk(
        n_tp, n_grp, qkv, cache_keys, cache_values, session_ids, cache_lens, owners,
        w_out, thinker_rows, talker_gain, w_talker,
    )


def solution(mesh):
    return jax.shard_map(
        on_device,
        mesh=mesh,
        in_specs=(
            P(("grp", "tp"), None),
            P(),
            P(None, "tp"),
            P(None, "tp"),
            P(None, "tp"),
            P("tp", None),
            P("grp", None, "tp"),
            P("grp", None, "tp"),
            P("grp", None),
            P("grp", None),
            P("grp", None),
            P(),
            P(None, "tp"),
        ),
        out_specs=P("grp", "tp"),
        check_vma=False,
    )
```

```python
import functools

import jax
import jax.numpy as jnp
from jax import lax
from jax.experimental import pallas as pl
from jax.experimental.pallas import tpu as pltpu
from jax.sharding import PartitionSpec as P

HEAD_DIM = 128
SESS = 16
CAPS = 2
GQA = 4
MOST = 20
OWNER_PITCH = 48
SLOT_PITCH = 24
CHUNKS = 8
VMEM_BYTES = 58 * 1024 * 1024

EPSILON = 1e-06
MESH = pl.DeviceIdType.MESH


def places(n_tp):
    me = lax.axis_index("tp")
    core = lax.rem(me, 2)
    chip = me // 2
    return me, chip, core, me + 1 - 2 * core


def greet(n_tp, n_grp=1):
    me, chip, core, sibling = places(n_tp)
    n_chips = n_tp // 2
    barrier = pltpu.get_barrier_semaphore()
    peers = [{"tp": sibling}]
    for j in range(1, n_chips):
        peers.append({"tp": lax.rem(chip + j, n_chips) * 2 + core})
    grp = lax.axis_index("grp")
    for j in range(1, n_grp):
        peers.append({"grp": lax.rem(grp + j, n_grp)})
    for peer in peers:
        pl.semaphore_signal(barrier, inc=1, device_id=peer, device_id_type=MESH)
    return functools.partial(pl.semaphore_wait, barrier, len(peers))


def remote(src, dst, send, recv, device):
    return pltpu.make_async_remote_copy(
        src_ref=src,
        dst_ref=dst,
        send_sem=send,
        recv_sem=recv,
        device_id=device,
        device_id_type=MESH,
    )


class RowGather:
    def __init__(self, n_tp, held, sib_send, chip_send, pass_send, recv):
        self.held, self.recv = held, recv
        self.sib_send, self.chip_send, self.pass_send = sib_send, chip_send, pass_send
        self.me, self.chip, self.core, self.sibling = places(n_tp)
        self.n_chips = n_tp // 2
        self.rows = held.shape[1] // n_tp

    def block(self, f, owner):
        start = pl.multiple_of(owner * self.rows, self.rows)
        return self.held.at[f, pl.ds(start, self.rows), :]

    def copy(self, f, owner, send, target):
        ref = self.block(f, owner)
        return remote(ref, ref, send, self.recv.at[f, owner], {"tp": target})

    def partner(self, j):
        return lax.rem(self.chip + j, self.n_chips) * 2 + self.core

    def own_copies(self, f):
        copies = [
            self.copy(f, self.me, self.chip_send.at[f, j - 1], self.partner(j))
            for j in range(1, self.n_chips)
        ]
        return copies + [self.copy(f, self.me, self.sib_send.at[f], self.sibling)]

    def passed_copies(self, f):
        return [
            self.copy(f, self.partner(j), self.pass_send.at[f, j - 1], self.sibling)
            for j in range(1, self.n_chips)
        ]

    def send(self, f):
        for copy in self.own_copies(f):
            copy.start()

    def pass_on(self, f):
        for copy in self.passed_copies(f):
            copy.wait_recv()
            copy.start()

    def wait_sibling(self, f):
        self.copy(f, self.sibling, self.sib_send.at[f], self.sibling).wait_recv()
        for j in range(1, self.n_chips):
            owner = lax.rem(self.chip + j, self.n_chips) * 2 + 1 - self.core
            self.copy(f, owner, self.pass_send.at[f, j - 1], self.sibling).wait_recv()

    def wait_sends(self, f):
        for copy in self.own_copies(f) + self.passed_copies(f):
            copy.wait_send()


def gather_scratch(n_tp, rows, width):
    other = max(1, n_tp // 2 - 1)
    return [
        pltpu.VMEM((CHUNKS, n_tp * rows, width), jnp.bfloat16),
        pltpu.SemaphoreType.DMA((CHUNKS,)),
        pltpu.SemaphoreType.DMA((CHUNKS, other)),
        pltpu.SemaphoreType.DMA((CHUNKS, other)),
        pltpu.SemaphoreType.DMA((CHUNKS, n_tp)),
    ]


def column_tile(columns):
    return 512 if columns % 512 == 0 else 256 if columns % 256 == 0 else 128


def project_kernel(
    n_tp, x_ref, gain_ref, wq_ref, wk_ref, wv_ref, out_ref,
    held, sib_send, chip_send, pass_send, recv, weights, total, w_sem,
):
    width = held.shape[2]
    model_width = width * CHUNKS
    edges = [0]
    for ref in (wq_ref, wk_ref, wv_ref):
        edges.append(edges[-1] + ref.shape[1])

    def weight_copies(f):
        start = pl.multiple_of(f * width, width)
        return [
            pltpu.make_async_copy(
                ref.at[pl.ds(start, width), :],
                weights.at[f, :, pl.ds(edges[i], ref.shape[1])],
                w_sem.at[f, i],
            )
            for i, ref in enumerate((wq_ref, wk_ref, wv_ref))
        ]

    def start_weights(f, carry):
        for copy in weight_copies(f):
            copy.start()
        return carry

    greeted = greet(n_tp)
    lax.fori_loop(0, CHUNKS, start_weights, 0)
    gather = RowGather(n_tp, held, sib_send, chip_send, pass_send, recv)

    def squares(f, carry):
        part = x_ref[:, pl.ds(pl.multiple_of(f * width, width), width)].astype(jnp.float32)
        return carry + jnp.sum(part * part, axis=1, keepdims=True)

    square_sum = lax.fori_loop(
        0, CHUNKS, squares, jnp.zeros((x_ref.shape[0], 1), jnp.float32)
    )
    scale = lax.rsqrt(square_sum / model_width + EPSILON)
    rows = gather.rows
    greeted()

    def normalise(f, carry):
        columns = pl.ds(pl.multiple_of(f * width, width), width)
        part = x_ref[:, columns].astype(jnp.float32) * scale
        part = part * gain_ref[columns][None, :].astype(jnp.float32)
        start = pl.multiple_of(gather.me * rows, rows)
        held[f, pl.ds(start, rows), :] = part.astype(jnp.bfloat16)
        gather.send(f)
        return carry

    lax.fori_loop(0, CHUNKS, normalise, 0)
    total[...] = jnp.zeros_like(total)
    tile = column_tile(total.shape[1])

    def step(f, carry):
        @pl.when(f < CHUNKS)
        def _():
            gather.pass_on(f)

        @pl.when(f >= 1)
        def _():
            g = f - 1
            gather.wait_sibling(g)
            for copy in weight_copies(g):
                copy.wait()
            for lower in range(0, total.shape[1], tile):
                total[:, lower : lower + tile] += jnp.dot(
                    held[g],
                    weights[g, :, lower : lower + tile],
                    preferred_element_type=jnp.float32,
                )

        return carry

    lax.fori_loop(0, CHUNKS + 1, step, 0)
    out_ref[...] = total[...].astype(jnp.bfloat16)

    def finish(f, carry):
        gather.wait_sends(f)
        return carry

    lax.fori_loop(0, CHUNKS, finish, 0)


def project(n_tp, rows_here, gain, w_query, w_key, w_value):
    rows, model_width = rows_here.shape
    width = model_width // CHUNKS
    columns = w_query.shape[1] + w_key.shape[1] + w_value.shape[1]
    vmem, hbm = pl.BlockSpec(memory_space=pltpu.VMEM), pl.BlockSpec(memory_space=pl.ANY)
    return pl.pallas_call(
        functools.partial(project_kernel, n_tp),
        out_shape=jax.ShapeDtypeStruct((n_tp * rows, columns), jnp.bfloat16),
        in_specs=[vmem, vmem, hbm, hbm, hbm],
        out_specs=vmem,
        scratch_shapes=gather_scratch(n_tp, rows, width)
        + [
            pltpu.VMEM((CHUNKS, width, columns), jnp.bfloat16),
            pltpu.VMEM((n_tp * rows, columns), jnp.float32),
            pltpu.SemaphoreType.DMA((CHUNKS, 3)),
        ],
        compiler_params=pltpu.CompilerParams(
            collective_id=0, has_side_effects=True, vmem_limit_bytes=VMEM_BYTES
        ),
        name="gather_project",
    )(rows_here, gain, w_query, w_key, w_value)


def slot_tables(ids_ref, owners_ref):
    ids = ids_ref[...]
    tokens = ids.shape[1]
    session = lax.broadcasted_iota(jnp.int32, (SESS, tokens), 0)
    member = (ids == session).astype(jnp.int32)
    starts = jnp.sum((ids < session).astype(jnp.int32), axis=1, keepdims=True)
    first = jnp.sum(member * starts, axis=0, keepdims=True)
    position = lax.broadcasted_iota(jnp.int32, (1, tokens), 1) - first
    one = lax.broadcasted_iota(jnp.int32, (SESS, SESS), 0)
    two = lax.broadcasted_iota(jnp.int32, (SESS, SESS), 1)
    named = owners_ref[...]
    owner = jnp.sum(jnp.where(one == two, named, 0), axis=1, keepdims=True)
    earlier = (owner == named) & (two < one)
    rank = jnp.sum(earlier.astype(jnp.int32), axis=1, keepdims=True)
    owner_slot = owner * OWNER_PITCH + rank * MOST
    destination = jnp.sum(member * owner_slot, axis=0, keepdims=True) + position
    return ids * SLOT_PITCH + position, destination


def attend(slot, qkv_ref, cache_copies, keys, values, lens_ref, slots, mixed, attended_ref):
    score_scale = HEAD_DIM ** (-0.5)
    n_cache = keys.shape[1]
    kv_local = keys.shape[2] // HEAD_DIM
    q_width = kv_local * GQA * HEAD_DIM
    kv_width = kv_local * HEAD_DIM
    slot_count = SESS * SLOT_PITCH
    slot_rows = lax.broadcasted_iota(jnp.int32, (slot_count, slot.shape[1]), 0)
    placing = (slot_rows == slot).astype(jnp.float32)
    tile = column_tile(slots.shape[1])
    for lower in range(0, slots.shape[1], tile):
        slots[:, lower : lower + tile] = jnp.dot(
            placing.astype(jnp.bfloat16),
            qkv_ref[:, lower : lower + tile],
            preferred_element_type=jnp.float32,
        )
    many = GQA * SLOT_PITCH
    cache_place = lax.broadcasted_iota(jnp.int32, (many, n_cache), 1)
    row = lax.broadcasted_iota(jnp.int32, (GQA, SLOT_PITCH, SLOT_PITCH), 1)
    column = lax.broadcasted_iota(jnp.int32, (GQA, SLOT_PITCH, SLOT_PITCH), 2)
    row, column = row.reshape(many, SLOT_PITCH), column.reshape(many, SLOT_PITCH)
    transposed = (((1,), (1,)), ((), ()))

    def scores(s, k):
        rows = pl.ds(pl.multiple_of(s * SLOT_PITCH, 8), SLOT_PITCH)
        heads = [slots[rows, pl.ds((k * GQA + g) * HEAD_DIM, HEAD_DIM)] for g in range(GQA)]
        query = jnp.concatenate(heads, axis=0).astype(jnp.bfloat16)
        key_new = slots[rows, pl.ds(q_width + k * HEAD_DIM, HEAD_DIM)].astype(jnp.bfloat16)
        cached = lax.dot_general(
            query,
            keys[s, :, pl.ds(k * HEAD_DIM, HEAD_DIM)],
            transposed,
            preferred_element_type=jnp.float32,
        )
        fresh = lax.dot_general(query, key_new, transposed, preferred_element_type=jnp.float32)
        return cached, fresh

    def masked(s, both):
        cached = jnp.where(cache_place < lens_ref[0, s], both[0] * score_scale, -1e30)
        return cached, jnp.where(column <= row, both[1] * score_scale, -1e30)

    def peak(both):
        return jnp.maximum(
            jnp.max(both[0], axis=1, keepdims=True), jnp.max(both[1], axis=1, keepdims=True)
        )

    def inverse_sum(both):
        return 1.0 / (
            jnp.sum(both[0], axis=1, keepdims=True) + jnp.sum(both[1], axis=1, keepdims=True)
        )

    def mix(s, k, weights):
        rows = pl.ds(pl.multiple_of(s * SLOT_PITCH, 8), SLOT_PITCH)
        lower = q_width + kv_width + k * HEAD_DIM
        value_new = slots[rows, pl.ds(lower, HEAD_DIM)].astype(jnp.bfloat16)
        sums = jnp.dot(
            weights[0],
            values[s, :, pl.ds(k * HEAD_DIM, HEAD_DIM)],
            preferred_element_type=jnp.float32,
        ) + jnp.dot(weights[1], value_new, preferred_element_type=jnp.float32)
        for g in range(GQA):
            mixed[rows, pl.ds((k * GQA + g) * HEAD_DIM, HEAD_DIM)] = sums[
                g * SLOT_PITCH : (g + 1) * SLOT_PITCH
            ]

    together = 4

    def sessions(i, carry):
        pairs = []
        for n in range(together):
            for copy in cache_copies(together * i + n):
                copy.wait()
            pairs.extend((together * i + n, k) for k in range(kv_local))
        dots = [scores(s, k) for s, k in pairs]
        dots = [masked(s, both) for (s, _), both in zip(pairs, dots)]
        peaks = [peak(both) for both in dots]
        powers = [
            (jnp.exp(cached - highest), jnp.exp(fresh - highest))
            for (cached, fresh), highest in zip(dots, peaks)
        ]
        inverses = [inverse_sum(both) for both in powers]
        weights = [
            ((cached * inverse).astype(jnp.bfloat16), (fresh * inverse).astype(jnp.bfloat16))
            for (cached, fresh), inverse in zip(powers, inverses)
        ]
        for (s, k), both in zip(pairs, weights):
            mix(s, k, both)
        return carry

    lax.fori_loop(0, SESS // together, sessions, 0)
    back = placing.T.astype(jnp.bfloat16)
    tile = column_tile(q_width)
    for lower in range(0, q_width, tile):
        attended_ref[:, lower : lower + tile] = jnp.dot(
            back,
            mixed[:, lower : lower + tile].astype(jnp.bfloat16),
            preferred_element_type=jnp.float32,
        ).astype(jnp.bfloat16)


def talk_kernel(
    n_tp, n_grp, qkv_ref, ck_ref, cv_ref, ids_ref, lens_ref, owners_ref,
    wo_ref, x_ref, gain_ref, wt_ref, out_ref,
    held, sib_send, chip_send, pass_send, recv,
    ordered, w_out, w_talk, kept, pair_out, pair_in, chip_out, chip_in,
    total, square_sum, owner_out, owner_in,
    keys, values, slots, mixed, attended_ref, cache_sem, wo_sem, wt_sem, pair_send, pair_recv, part_send, part_recv, owner_send, owner_recv,
):
    width = held.shape[2]
    model_width = width * CHUNKS
    head_width = GQA * HEAD_DIM

    def weight_copies(f):
        start = pl.multiple_of(f * width, width)
        return (
            pltpu.make_async_copy(wo_ref.at[:, pl.ds(start, width)], w_out.at[f], wo_sem.at[f]),
            pltpu.make_async_copy(wt_ref.at[pl.ds(start, width), :], w_talk.at[f], wt_sem.at[f]),
        )

    def start_weights(which):
        def body(f, carry):
            weight_copies(f)[which].start()
            return carry

        lax.fori_loop(0, CHUNKS, body, 0)

    def cache_copies(s):
        return (
            pltpu.make_async_copy(ck_ref.at[s], keys.at[s], cache_sem.at[s, 0]),
            pltpu.make_async_copy(cv_ref.at[s], values.at[s], cache_sem.at[s, 1]),
        )

    def start_cache(s, carry):
        for copy in cache_copies(s):
            copy.start()
        return carry

    greeted = greet(n_tp, n_grp)
    lax.fori_loop(0, SESS, start_cache, 0)
    start_weights(0)
    start_weights(1)
    slot, destination = slot_tables(ids_ref, owners_ref)
    attend(slot, qkv_ref, cache_copies, keys, values, lens_ref, slots, mixed, attended_ref)
    gather = RowGather(n_tp, held, sib_send, chip_send, pass_send, recv)
    me, chip, core, sibling = gather.me, gather.chip, gather.core, gather.sibling
    n_chips, rows = gather.n_chips, gather.rows
    half = n_chips * rows
    for c in range(n_chips):
        for side, owner in enumerate((2 * c + 1 - core, 2 * c + core)):
            ordered[side * half + c * rows : side * half + (c + 1) * rows, :] = attended_ref[
                pl.ds(pl.multiple_of(owner * rows, rows), rows), :
            ]
    greeted()

    def pair_copy(f):
        return remote(
            pair_out.at[f], pair_in.at[f], pair_send.at[f], pair_recv.at[f], {"tp": sibling}
        )

    def part_copy(f, j):
        return remote(
            chip_out.at[f, j - 1],
            chip_in.at[f, j - 1],
            part_send.at[f, j - 1],
            part_recv.at[f, j - 1],
            {"tp": gather.partner(j)},
        )

    tile = column_tile(width)

    def reduce_step(f, carry):
        @pl.when(f < CHUNKS)
        def _():
            weight_copies(f)[0].wait()
            for lower in range(0, width, tile):
                summed = None
                for first in range(0, ordered.shape[1], head_width):
                    part = jnp.dot(
                        ordered[:, first : first + head_width],
                        w_out[f, first : first + head_width, lower : lower + tile],
                        preferred_element_type=jnp.float32,
                    )
                    part = part.astype(jnp.bfloat16).astype(jnp.float32)
                    summed = part if summed is None else summed + part
                pair_out[f, :, lower : lower + tile] = summed[:half].astype(jnp.bfloat16)
                kept[f, :, lower : lower + tile] = summed[half:]
            pair_copy(f).start()

        @pl.when(f >= 1)
        def _():
            g = f - 1
            pair_copy(g).wait_recv()
            for j in range(1, n_chips):
                there = pl.ds(pl.multiple_of(lax.rem(chip + j, n_chips) * rows, rows), rows)
                both = kept[g, there, :] + pair_in[g, there, :].astype(jnp.float32)
                chip_out[g, j - 1] = both.astype(jnp.bfloat16)
                part_copy(g, j).start()

        return carry

    lax.fori_loop(0, CHUNKS + 1, reduce_step, 0)

    def hidden_step(f, carry):
        here = pl.ds(pl.multiple_of(chip * rows, rows), rows)
        both = kept[f, here, :] + pair_in[f, here, :].astype(jnp.float32)
        for j in range(1, n_chips):
            part_copy(f, j).wait_recv()
            both = both + chip_in[f, j - 1].astype(jnp.float32)
        columns = pl.ds(pl.multiple_of(f * width, width), width)
        hidden = x_ref[:, columns].astype(jnp.float32) + both
        held[f, pl.ds(pl.multiple_of(me * rows, rows), rows), :] = hidden.astype(jnp.bfloat16)
        gather.send(f)
        return carry

    lax.fori_loop(0, CHUNKS, hidden_step, 0)
    total[...] = jnp.zeros_like(total)
    square_sum[...] = jnp.zeros_like(square_sum)

    def talk_step(f, carry):
        @pl.when(f < CHUNKS)
        def _():
            gather.pass_on(f)

        @pl.when(f >= 1)
        def _():
            g = f - 1
            gather.wait_sibling(g)
            weight_copies(g)[1].wait()
            hidden = held[g].astype(jnp.float32)
            square_sum[...] += jnp.sum(hidden * hidden, axis=1, keepdims=True)
            columns = pl.ds(pl.multiple_of(g * width, width), width)
            gained = (hidden * gain_ref[columns][None, :].astype(jnp.float32)).astype(jnp.bfloat16)
            total[...] += jnp.dot(gained, w_talk[g], preferred_element_type=jnp.float32)

        return carry

    lax.fori_loop(0, CHUNKS + 1, talk_step, 0)
    scale = lax.rsqrt(square_sum[...] / model_width + EPSILON)
    talk = (total[...] * scale).astype(jnp.bfloat16)
    pitch = owner_out.shape[1]
    grp = lax.axis_index("grp")

    def owner_copy(j):
        target = lax.rem(grp + j, n_grp)
        return remote(
            owner_out.at[target],
            owner_in.at[grp],
            owner_send.at[j],
            owner_recv.at[grp],
            {"grp": target},
        )

    def owner_arrival(j):
        source = lax.rem(grp + n_grp - j, n_grp)
        return remote(
            owner_out.at[source],
            owner_in.at[source],
            owner_send.at[j],
            owner_recv.at[source],
            {"grp": source},
        )

    routing_rows = lax.broadcasted_iota(jnp.int32, (n_grp * pitch, talk.shape[0]), 0)
    routing = (routing_rows == destination).astype(jnp.float32).astype(jnp.bfloat16)
    routed = jnp.dot(routing, talk, preferred_element_type=jnp.float32)
    for o in range(n_grp):
        owner_out[o] = routed[o * pitch : (o + 1) * pitch].astype(jnp.bfloat16)
    for j in range(1, n_grp):
        owner_copy(j).start()
    owner_in[grp] = owner_out[grp]
    for j in range(1, n_grp):
        owner_arrival(j).wait_recv()
    used = CAPS * MOST
    out_ref[...] = jnp.concatenate(
        [owner_in[o].astype(jnp.float32)[:used] for o in range(n_grp)], axis=0
    ).astype(jnp.bfloat16)

    def finish(f, carry):
        gather.wait_sends(f)
        pair_copy(f).wait_send()
        for j in range(1, n_chips):
            part_copy(f, j).wait_send()
        return carry

    lax.fori_loop(0, CHUNKS, finish, 0)
    for j in range(1, n_grp):
        owner_copy(j).wait_send()


def talk(
    n_tp, n_grp, qkv, cache_keys, cache_values, session_ids, cache_lens, owners,
    w_out, rows_here, gain, w_talker,
):
    rows, model_width = rows_here.shape
    width = model_width // CHUNKS
    columns = w_talker.shape[1]
    other = max(1, n_tp // 2 - 1)
    half = n_tp // 2 * rows
    pitch = OWNER_PITCH
    slot_count = SESS * SLOT_PITCH
    q_width = w_out.shape[0]
    vmem, hbm = pl.BlockSpec(memory_space=pltpu.VMEM), pl.BlockSpec(memory_space=pl.ANY)
    smem = pl.BlockSpec(memory_space=pltpu.SMEM)
    bf16, dma = jnp.bfloat16, pltpu.SemaphoreType.DMA
    return pl.pallas_call(
        functools.partial(talk_kernel, n_tp, n_grp),
        out_shape=jax.ShapeDtypeStruct((n_grp * CAPS * MOST, columns), bf16),
        in_specs=[vmem, hbm, hbm, vmem, smem, vmem, hbm, vmem, vmem, hbm],
        out_specs=vmem,
        scratch_shapes=gather_scratch(n_tp, rows, width)
        + [
            pltpu.VMEM((n_tp * rows, q_width), bf16),
            pltpu.VMEM((CHUNKS, w_out.shape[0], width), bf16),
            pltpu.VMEM((CHUNKS, width, columns), bf16),
            pltpu.VMEM((CHUNKS, half, width), jnp.float32),
            pltpu.VMEM((CHUNKS, half, width), bf16),
            pltpu.VMEM((CHUNKS, half, width), bf16),
            pltpu.VMEM((CHUNKS, other, rows, width), bf16),
            pltpu.VMEM((CHUNKS, other, rows, width), bf16),
            pltpu.VMEM((n_tp * rows, columns), jnp.float32),
            pltpu.VMEM((n_tp * rows, 1), jnp.float32),
            pltpu.VMEM((n_grp, pitch, columns), bf16),
            pltpu.VMEM((n_grp, pitch, columns), bf16),
            pltpu.VMEM(cache_keys.shape, bf16),
            pltpu.VMEM(cache_values.shape, bf16),
            pltpu.VMEM((slot_count, qkv.shape[1]), jnp.float32),
            pltpu.VMEM((slot_count, q_width), jnp.float32),
            pltpu.VMEM((n_tp * rows, q_width), bf16),
            dma((SESS, 2)),
            dma((CHUNKS,)),
            dma((CHUNKS,)),
            dma((CHUNKS,)),
            dma((CHUNKS,)),
            dma((CHUNKS, other)),
            dma((CHUNKS, other)),
            dma((n_grp,)),
            dma((n_grp,)),
        ],
        compiler_params=pltpu.CompilerParams(
            collective_id=1, has_side_effects=True, vmem_limit_bytes=VMEM_BYTES
        ),
        name="attend_talk",
    )(
        qkv, cache_keys, cache_values, session_ids, cache_lens, owners.reshape(1, SESS),
        w_out, rows_here, gain, w_talker,
    )


def on_device(
    thinker_rows,
    norm_gain,
    w_query,
    w_key,
    w_value,
    w_out,
    cache_keys,
    cache_values,
    session_ids,
    cache_lens,
    owners,
    talker_gain,
    w_talker,
):
    n_tp, n_grp = lax.axis_size("tp"), lax.axis_size("grp")
    qkv = project(n_tp, thinker_rows, norm_gain, w_query, w_key, w_value)
    return talk(
        n_tp, n_grp, qkv, cache_keys, cache_values, session_ids, cache_lens, owners,
        w_out, thinker_rows, talker_gain, w_talker,
    )


def solution(mesh):
    return jax.shard_map(
        on_device,
        mesh=mesh,
        in_specs=(
            P(("grp", "tp"), None),
            P(),
            P(None, "tp"),
            P(None, "tp"),
            P(None, "tp"),
            P("tp", None),
            P("grp", None, "tp"),
            P("grp", None, "tp"),
            P("grp", None),
            P("grp", None),
            P("grp", None),
            P(),
            P(None, "tp"),
        ),
        out_specs=P("grp", "tp"),
        check_vma=False,
    )
```
